512 devices in a mesh: row: 4 (over x_hi, core), col: 16 (over z, x_lo), rep: 8 (over y).
Axes of the slice: x: 4 (x_hi: 2, x_lo: 2; x = x_hi * 2 + x_lo), y: 8, z: 8, core: 2. Of those that a mesh axis runs over, the one named last changes fastest.
Arguments:
- amplitudes: bfloat16 [1024, 327680], P(('row', 'col', 'rep')), may hold values from -24 to 24
- integrals: bfloat16 [327680, 1024], P(('col', 'rep'), 'row'), may hold values from -0.009765625 to 0.009765625
Outputs:
- ladder: float32 [1024, 1024], P(('row', 'col', 'rep'))
The draws below stay inside these ranges and needn't reach their ends.
All inputs are finite; a program needn't handle non-finite values.
Results may differ from the reference program's by a relative error of at most 0.0003.
Values may be sent and summed in bfloat16 or wider, within the bound.
No kernel may reach another device: no remote copies, remote signals or barrier semaphores. Data moves between devices by JAX's collectives and lax.ppermute only.
A program may use at most 64 MiB of HBM per device.

```python
import jax
import jax.numpy as jnp

CD = 327680
NAB = 1024
IJ = 1024


def spiked(values, stream_key, source, target, shards_of, factor):
    owner, partner = [(jnp.arange(values.shape[axis_at]) // (values.shape[axis_at] // shards_of)).reshape([-1 if axis == axis_at else 1 for axis in range(values.ndim)]) for axis_at in (source, target)]
    chosen = jax.random.permutation(stream_key, shards_of)[partner]
    strong = (owner == chosen) | (owner == (partner + shards_of // 2) % shards_of)
    return jnp.where(strong, factor * values, values)


def level_of(stream_key, shape, split, least, top_value):
    loudness = 1.0
    for position, parts in split:
        steps = jax.random.uniform(jax.random.fold_in(jax.random.fold_in(stream_key, 6), position), (parts,), jnp.float32, least / len(split), top_value / len(split))
        loudness = loudness * jnp.repeat(jnp.exp(steps), shape[position] // parts).reshape((-1,) + (1,) * (len(shape) - 1 - position))
    return loudness


def scatter_about(own_key, extent, spread, limit, shards=(), dtype=jnp.bfloat16):
    loudness = level_of(own_key, extent, shards, -0.22, 0.18) if shards else 1.0
    result = jax.random.normal(own_key, extent, jnp.float32) * spread * loudness
    return jnp.minimum(jnp.maximum(result, -limit), limit).astype(dtype)


def heavy_noise(rng, extent, deviation, bound, pieces, heavy, held_as=jnp.bfloat16):
    values = deviation * jax.random.normal(rng, extent, jnp.float32)
    if pieces:
        values = values * level_of(rng, extent, pieces, -0.22, 0.18)
    return jnp.clip(spiked(values, jax.random.fold_in(rng, 3), *heavy), -bound, bound).astype(held_as)


def setup_inputs(seed: int = 0) -> dict:
    arg_keys = jax.random.split(jax.random.key(seed), 3)
    amplitudes = heavy_noise(arg_keys[0], (IJ, CD), 1.0, 24.0, ((0, 512),), (1, 0, 512, 6.0))
    integrals = scatter_about(arg_keys[1], (CD, NAB), CD ** -0.5, 0.009765625, ((0, 128), (1, 4)))
    return {"amplitudes": amplitudes, "integrals": integrals}


def reference(amplitudes, integrals):
    contracted = jnp.dot(amplitudes, integrals, preferred_element_type=jnp.float32)
    return 0.5 * contracted
```

```python
import jax
import jax.numpy as jnp
from jax import lax
from jax.sharding import Mesh, PartitionSpec as P


def pairs(a, b):
    moves = []
    for xh in range(2):
        for core in range(2):
            for xl in range(2):
                source = (xh * 2 + core) * 2 + xl
                target = ((xh ^ a) * 2 + xl) * 2 + (core ^ b)
                moves.append((source, target))
    return moves


def shards(amplitudes, integrals):
    pieces = [lax.ppermute(integrals, ("xh", "core", "xl"), pairs(a, b)) for a, b in ((1, 0), (1, 1), (0, 0), (0, 1))]
    blocks = lax.all_to_all(amplitudes, ("z", "core", "y"), split_axis=1, concat_axis=0, tiled=True)
    far0, far1, near0, near1 = [jnp.dot(blocks, p, preferred_element_type=jnp.float32) for p in pieces]
    core, xh, xl = lax.axis_index("core"), lax.axis_index("xh"), lax.axis_index("xl")
    partial = jnp.concatenate([near0, near1, far0, far1], axis=1).reshape(8, 2, 16, 1024)
    mine = lax.dynamic_index_in_dim(partial, core, 1, False)
    other = lax.dynamic_index_in_dim(partial, 1 - core, 1, False)
    both = mine + lax.ppermute(other, "core", [(0, 1), (1, 0)])
    parts = lax.all_to_all(both.reshape(128, 1024), ("z", "y"), split_axis=0, concat_axis=0, tiled=True)
    total = 0.5 * parts.reshape(64, 2, 1024).sum(0)
    total = total.reshape(2, 2, 2, 256)
    total = jnp.where(xh == 1, total[:, ::-1], total)
    total = jnp.where(xl == 1, total[:, :, ::-1], total)
    return total.reshape(2, 1024)


def solution(mesh):
    fine = Mesh(mesh.devices.reshape(2, 2, 8, 2, 8), ("xh", "core", "z", "xl", "y"))
    rows = P(("xh", "core", "z", "xl", "y"), None)
    in_specs = (rows, P(("z", "xl", "y"), ("xh", "core")))
    return jax.shard_map(shards, mesh=fine, in_specs=in_specs, out_specs=rows, check_vma=False)
```

```python
import jax
import jax.numpy as jnp
from jax import lax
from jax.experimental import pallas as pl
from jax.experimental.pallas import tpu as pltpu
from jax.sharding import Mesh, PartitionSpec as P

RING = ("xh", "xl")
RIGHT = [(i, (i + 1) % 4) for i in range(4)]
LEFT = [(i, (i + 3) % 4) for i in range(4)]
SWAP = [(0, 1), (1, 0)]
VMEM = pl.BlockSpec(memory_space=pltpu.VMEM)
ANY = pl.BlockSpec(memory_space=pl.ANY)


def fetch(across, blocks, held, sems):
    core, xh, xl = lax.axis_index("core"), lax.axis_index("xh"), lax.axis_index("xl")
    here, left, right, far_top, far_low = blocks
    wanted = 1 - core if across else core

    @pl.when(xl == wanted)
    def _():
        pltpu.make_async_copy(here, held.at[xh], sems.at[xh]).start()
        pltpu.make_async_copy(far_top, held.at[1 - xh, :1280], sems.at[1 - xh]).start()
        pltpu.make_async_copy(far_low, held.at[1 - xh, 1280:], sems.at[1 - xh]).start()

    @pl.when(xl != wanted)
    def _():
        pltpu.make_async_copy(right, held.at[lax.rem(xh + xl, 2)], sems.at[lax.rem(xh + xl, 2)]).start()
        pltpu.make_async_copy(left, held.at[lax.rem(xh + 1 - xl, 2)], sems.at[lax.rem(xh + 1 - xl, 2)]).start()

    return [pltpu.make_async_copy(here, held.at[place], sems.at[place]) for place in range(2)]


def first_half(rows_ref, here, left, right, far_top, far_low, sum_ref, held, sems):
    copies = fetch(False, (here, left, right, far_top, far_low), held, sems)
    for xh in range(2):
        copies[xh].wait()
        sum_ref[:, 256 * xh : 256 * xh + 256] = jnp.dot(rows_ref[...], held[xh], preferred_element_type=jnp.float32)


def second_half(sum_ref, rows_ref, here, left, right, far_top, far_low, mine_ref, theirs_ref, held, sems):
    core = lax.axis_index("core")
    copies = fetch(True, (here, left, right, far_top, far_low), held, sems)
    for xh in range(2):
        copies[xh].wait()
        total = jnp.dot(rows_ref[...], held[xh], preferred_element_type=jnp.float32)
        total = total + sum_ref[:, 256 * xh : 256 * xh + 256]
        total = total.reshape(8, 2, 16, 256)
        first, second = total[:, 0].reshape(128, 256), total[:, 1].reshape(128, 256)
        mine = jnp.where(core == 0, first, second)
        theirs = jnp.where(core == 0, second, first)
        for half in range(2):
            place = pl.ds(2 * xh + half, 128, stride=4)
            mine_ref[place, :] = mine[:, 128 * half : 128 * half + 128]
            theirs_ref[place, :] = theirs[:, 128 * half : 128 * half + 128]


def call(kernel, n_vmem, shapes):
    return pl.pallas_call(
        kernel,
        out_shape=[jax.ShapeDtypeStruct(shape, jnp.float32) for shape in shapes],
        in_specs=[VMEM] * n_vmem + [ANY] * 5,
        out_specs=[VMEM] * len(shapes),
        scratch_shapes=[pltpu.VMEM((2, 2560, 256), jnp.bfloat16), pltpu.SemaphoreType.DMA((2,))],
        compiler_params=pltpu.CompilerParams(vmem_limit_bytes=LIMIT),
        cost_estimate=pl.CostEstimate(flops=FLOPS, bytes_accessed=2**22, transcendentals=0),
    )


def halves(left, right, top_ref, low_ref, sems):
    top = pltpu.make_async_copy(left.at[:1280], top_ref, sems.at[0])
    low = pltpu.make_async_copy(right.at[1280:], low_ref, sems.at[1])
    top.start()
    low.start()
    top.wait()
    low.wait()


def halved(left, right):
    return pl.pallas_call(
        halves,
        out_shape=[jax.ShapeDtypeStruct((1280, 256), jnp.bfloat16)] * 2,
        in_specs=[ANY, ANY],
        out_specs=[ANY, ANY],
        scratch_shapes=[pltpu.SemaphoreType.DMA((2,))],
        compiler_params=pltpu.CompilerParams(vmem_limit_bytes=LIMIT),
        cost_estimate=pl.CostEstimate(flops=G_FLOPS, bytes_accessed=2**21, transcendentals=0),
    )(left, right)


G_FLOPS = 4 * 10**10
LIMIT = 16 * 2**20
FLOPS = 4 * 10**10


def shards(amplitudes, integrals):
    core = lax.axis_index("core")
    left = lax.ppermute(integrals, RING, RIGHT)
    right = lax.ppermute(integrals, RING, LEFT)
    far_from = halved(left, right)
    far_top = lax.ppermute(far_from[0], RING, RIGHT)
    far_low = lax.ppermute(far_from[1], RING, LEFT)
    blocks = (integrals, left, right, far_top, far_low)
    own = lax.all_to_all(amplitudes, ("z", "core", "y"), split_axis=1, concat_axis=0, tiled=True)
    own, _, _ = lax.optimization_barrier((own, *far_from))
    other = lax.ppermute(own, "core", SWAP)
    (half_sum,) = call(first_half, 1, [(256, 512)])(own, *blocks)
    mine, theirs = call(second_half, 2, [(512, 128)] * 2)(half_sum, other, *blocks)
    got = lax.ppermute(theirs, "core", SWAP)
    mine, got = mine.reshape(64, 8, 128), got.reshape(64, 8, 128)
    first, second = jnp.where(core == 0, mine, got), jnp.where(core == 0, got, mine)
    partial = jnp.concatenate([first, second], axis=1)
    parts = lax.all_to_all(partial, ("z", "y"), split_axis=0, concat_axis=0, tiled=True)
    total = 0.5 * jnp.sum(parts, axis=0)
    return total.reshape(2, 2, 2, 256).transpose(1, 2, 0, 3).reshape(2, 1024)


def solution(mesh):
    fine = Mesh(mesh.devices.reshape(2, 2, 8, 2, 8), ("xh", "core", "z", "xl", "y"))
    rows = P(("xh", "core", "z", "xl", "y"), None)
    in_specs = (rows, P(("z", "xl", "y"), ("xh", "core")))
    return jax.shard_map(shards, mesh=fine, in_specs=in_specs, out_specs=rows, check_vma=False)
```

```python
import jax
import jax.numpy as jnp
from jax import lax
from jax.experimental import pallas as pl
from jax.experimental.pallas import tpu as pltpu
from jax.sharding import Mesh, PartitionSpec as P

RING = ("xh", "xl")
RIGHT = [(i, (i + 1) % 4) for i in range(4)]
LEFT = [(i, (i + 3) % 4) for i in range(4)]
SWAP = [(0, 1), (1, 0)]
VMEM = pl.BlockSpec(memory_space=pltpu.VMEM)
LIMIT = 20 * 2**20
H_LIMIT = 8 * 2**20
G_FLOPS = 2 * 10**10
FLOPS = 10**11


def keep(first, second, first_ref, second_ref):
    first_ref[...] = first[...]
    second_ref[...] = second[...]


def kept(first, second):
    return pl.pallas_call(
        keep,
        out_shape=[jax.ShapeDtypeStruct(first.shape, first.dtype)] * 2,
        in_specs=[VMEM, VMEM],
        out_specs=[VMEM, VMEM],
        compiler_params=pltpu.CompilerParams(vmem_limit_bytes=H_LIMIT),
        cost_estimate=pl.CostEstimate(flops=G_FLOPS, bytes_accessed=2**21, transcendentals=0),
    )(first, second)


def halves(blocks, top_ref, low_ref):
    top_ref[...] = blocks[:1280]
    low_ref[...] = blocks[1280:]


def halved(blocks):
    return pl.pallas_call(
        halves,
        out_shape=[jax.ShapeDtypeStruct((1280, 256), jnp.bfloat16)] * 2,
        in_specs=[VMEM],
        out_specs=[VMEM, VMEM],
        compiler_params=pltpu.CompilerParams(vmem_limit_bytes=H_LIMIT),
    )(blocks)


def multiply(across, rows, blocks, sum_ref):
    core, xh, xl = lax.axis_index("core"), lax.axis_index("xh"), lax.axis_index("xl")
    here, left, right, far = blocks[:2], blocks[2:4], blocks[4:6], blocks[6:]
    wanted = 1 - core if across else core

    def dot(halves):
        top = jnp.dot(rows[:, :1280], halves[0][...], preferred_element_type=jnp.float32)
        return top + jnp.dot(rows[:, 1280:], halves[1][...], preferred_element_type=jnp.float32)

    @pl.when(xl == wanted)
    def _():
        sum_ref[xh] = dot(here)
        sum_ref[1 - xh] = dot(far)

    @pl.when(xl != wanted)
    def _():
        sum_ref[lax.rem(xh + xl, 2)] = dot(right)
        sum_ref[lax.rem(xh + 1 - xl, 2)] = dot(left)


def first_half(pieces, *refs):
    *blocks, sum_ref, rows = refs
    rows[...] = pieces[...].reshape(256, 2560)
    multiply(False, rows, blocks, sum_ref)


def second_half(first_ref, pieces, *refs):
    *blocks, mine_ref, theirs_ref, rows, sum_ref = refs
    core = lax.axis_index("core")
    rows[...] = pieces[...].reshape(256, 2560)
    multiply(True, rows, blocks, sum_ref)
    for xh in range(2):
        total = (first_ref[xh] + sum_ref[xh]).reshape(8, 2, 16, 256)
        first, second = total[:, 0].reshape(128, 256), total[:, 1].reshape(128, 256)
        mine = jnp.where(core == 0, first, second)
        theirs = jnp.where(core == 0, second, first)
        for half in range(2):
            place = pl.ds(2 * xh + half, 128, stride=4)
            mine_ref[place, :] = mine[:, 128 * half : 128 * half + 128]
            theirs_ref[place, :] = theirs[:, 128 * half : 128 * half + 128]


def first_sums(pieces, *blocks):
    return pl.pallas_call(
        first_half,
        out_shape=jax.ShapeDtypeStruct((2, 256, 256), jnp.float32),
        in_specs=[VMEM] * 9,
        out_specs=VMEM,
        scratch_shapes=[pltpu.VMEM((256, 2560), jnp.bfloat16)],
        compiler_params=pltpu.CompilerParams(vmem_limit_bytes=LIMIT),
        cost_estimate=pl.CostEstimate(flops=FLOPS, bytes_accessed=2**22, transcendentals=0),
    )(pieces, *blocks)


def second_sums(first, pieces, *blocks):
    return pl.pallas_call(
        second_half,
        out_shape=[jax.ShapeDtypeStruct((512, 128), jnp.float32)] * 2,
        in_specs=[VMEM] * 10,
        out_specs=[VMEM] * 2,
        scratch_shapes=[pltpu.VMEM((256, 2560), jnp.bfloat16), pltpu.VMEM((2, 256, 256), jnp.float32)],
        compiler_params=pltpu.CompilerParams(vmem_limit_bytes=LIMIT),
        cost_estimate=pl.CostEstimate(flops=10**9, bytes_accessed=2**22, transcendentals=0),
    )(first, pieces, *blocks)


def shards(amplitudes, integrals):
    core = lax.axis_index("core")
    top, low = halved(integrals)
    left_top = lax.ppermute(top, RING, RIGHT)
    right_low = lax.ppermute(low, RING, LEFT)
    left_low = lax.ppermute(low, RING, RIGHT)
    right_top = lax.ppermute(top, RING, LEFT)
    left_top, right_low = kept(left_top, right_low)
    far_top = lax.ppermute(left_top, RING, RIGHT)
    far_low = lax.ppermute(right_low, RING, LEFT)
    raw = lax.all_to_all(amplitudes.reshape(2, 128, 2560), ("z", "core", "y"), split_axis=1, concat_axis=1, tiled=True)
    raw, _, _ = lax.optimization_barrier((raw, left_top, right_low))
    raw_other = lax.ppermute(raw, "core", SWAP)
    blocks = (top, low, left_top, left_low, right_top, right_low, far_top, far_low)
    first = first_sums(raw.transpose(1, 0, 2), *blocks)
    mine, theirs = second_sums(first, raw_other.transpose(1, 0, 2), *blocks)
    got = lax.ppermute(theirs, "core", SWAP)
    mine, got = mine.reshape(64, 8, 128), got.reshape(64, 8, 128)
    first, second = jnp.where(core == 0, mine, got), jnp.where(core == 0, got, mine)
    partial = jnp.concatenate([first, second], axis=1)
    parts = lax.all_to_all(partial, ("z", "y"), split_axis=0, concat_axis=0, tiled=True)
    total = 0.5 * jnp.sum(parts, axis=0)
    return total.reshape(2, 2, 2, 256).transpose(1, 2, 0, 3).reshape(2, 1024)


def solution(mesh):
    fine = Mesh(mesh.devices.reshape(2, 2, 8, 2, 8), ("xh", "core", "z", "xl", "y"))
    rows = P(("xh", "core", "z", "xl", "y"), None)
    in_specs = (rows, P(("z", "xl", "y"), ("xh", "core")))
    return jax.shard_map(shards, mesh=fine, in_specs=in_specs, out_specs=rows, check_vma=False)
```

```python
import jax
import jax.numpy as jnp
from jax import lax
from jax.experimental import pallas as pl
from jax.experimental.pallas import tpu as pltpu
from jax.sharding import Mesh, PartitionSpec as P

RING = ("xh", "xl")
RIGHT = [(i, (i + 1) % 4) for i in range(4)]
LEFT = [(i, (i + 3) % 4) for i in range(4)]
SWAP = [(0, 1), (1, 0)]
VMEM = pl.BlockSpec(memory_space=pltpu.VMEM)
LIMIT = 20 * 2**20
H_LIMIT = 8 * 2**20
SPLIT = 2048
G_FLOPS = 10**10
B_FLOPS = 10**10
FLOPS = 10**11


def keep(*refs):
    for source, target in zip(refs[: len(refs) // 2], refs[len(refs) // 2 :]):
        target[...] = source[...]


def kept(flops, *pieces):
    return pl.pallas_call(
        keep,
        out_shape=[jax.ShapeDtypeStruct(piece.shape, piece.dtype) for piece in pieces],
        in_specs=[VMEM] * len(pieces),
        out_specs=[VMEM] * len(pieces),
        compiler_params=pltpu.CompilerParams(vmem_limit_bytes=H_LIMIT),
        cost_estimate=pl.CostEstimate(flops=flops, bytes_accessed=2**21, transcendentals=0),
    )(*pieces)


def halves(blocks, top_ref, low_ref):
    top_ref[...] = blocks[:SPLIT]
    low_ref[...] = blocks[SPLIT:]


def halved(blocks):
    return pl.pallas_call(
        halves,
        out_shape=[jax.ShapeDtypeStruct((rows, 256), jnp.bfloat16) for rows in (SPLIT, 2560 - SPLIT)],
        in_specs=[VMEM],
        out_specs=[VMEM, VMEM],
        compiler_params=pltpu.CompilerParams(vmem_limit_bytes=H_LIMIT),
    )(blocks)


def multiply(across, rows, blocks, sum_ref):
    core, xh, xl = lax.axis_index("core"), lax.axis_index("xh"), lax.axis_index("xl")
    here, left, right, far = blocks[:2], blocks[2:4], blocks[4:6], blocks[6:]
    wanted = 1 - core if across else core

    def dot(halves):
        top = jnp.dot(rows[:, :SPLIT], halves[0][...], preferred_element_type=jnp.float32)
        return top + jnp.dot(rows[:, SPLIT:], halves[1][...], preferred_element_type=jnp.float32)

    @pl.when(xl == wanted)
    def _():
        sum_ref[xh] = dot(here)
        sum_ref[1 - xh] = dot(far)

    @pl.when(xl != wanted)
    def _():
        sum_ref[lax.rem(xh + xl, 2)] = dot(right)
        sum_ref[lax.rem(xh + 1 - xl, 2)] = dot(left)


def first_half(pieces, *refs):
    *blocks, sum_ref, rows = refs
    rows[...] = pieces[...].reshape(256, 2560)
    multiply(False, rows, blocks, sum_ref)


def second_half(first_ref, pieces, *refs):
    *blocks, out_ref, rows, sum_ref = refs
    rows[...] = pieces[...].reshape(256, 2560)
    multiply(True, rows, blocks, sum_ref)
    for xh in range(2):
        total = first_ref[xh] + sum_ref[xh]
        for half in range(2):
            out_ref[pl.ds(2 * xh + half, 256, stride=4), :] = total[:, 128 * half : 128 * half + 128]


def first_sums(pieces, *blocks):
    return pl.pallas_call(
        first_half,
        out_shape=jax.ShapeDtypeStruct((2, 256, 256), jnp.float32),
        in_specs=[VMEM] * 9,
        out_specs=VMEM,
        scratch_shapes=[pltpu.VMEM((256, 2560), jnp.bfloat16)],
        compiler_params=pltpu.CompilerParams(vmem_limit_bytes=LIMIT),
        cost_estimate=pl.CostEstimate(flops=FLOPS, bytes_accessed=2**22, transcendentals=0),
    )(pieces, *blocks)


def second_sums(first, pieces, *blocks):
    return pl.pallas_call(
        second_half,
        out_shape=jax.ShapeDtypeStruct((1024, 128), jnp.float32),
        in_specs=[VMEM] * 10,
        out_specs=VMEM,
        scratch_shapes=[pltpu.VMEM((256, 2560), jnp.bfloat16), pltpu.VMEM((2, 256, 256), jnp.float32)],
        compiler_params=pltpu.CompilerParams(vmem_limit_bytes=LIMIT),
        cost_estimate=pl.CostEstimate(flops=10**9, bytes_accessed=2**22, transcendentals=0),
    )(first, pieces, *blocks)


def shards(amplitudes, integrals):
    top, low = halved(integrals)
    left_top = lax.ppermute(top, RING, RIGHT)
    right_low = lax.ppermute(low, RING, LEFT)
    left_low = lax.ppermute(low, RING, RIGHT)
    right_top = lax.ppermute(top, RING, LEFT)
    (left_top,) = kept(G_FLOPS, left_top)
    (right_low,) = kept(B_FLOPS, right_low)
    far_top = lax.ppermute(left_top, RING, RIGHT)
    far_low = lax.ppermute(right_low, RING, LEFT)
    raw = lax.all_to_all(amplitudes.reshape(2, 128, 2560), ("z", "core", "y"), split_axis=1, concat_axis=1, tiled=True)
    raw, _, _ = lax.optimization_barrier((raw, left_top, right_low))
    raw_other = lax.ppermute(raw, "core", SWAP)
    blocks = (top, low, left_top, left_low, right_top, right_low, far_top, far_low)
    first = first_sums(raw.transpose(1, 0, 2), *blocks)
    partial = second_sums(first, raw_other.transpose(1, 0, 2), *blocks).reshape(128, 8, 128)
    parts = lax.all_to_all(partial, ("z", "core", "y"), split_axis=0, concat_axis=0, tiled=True)
    total = 0.5 * jnp.sum(parts.reshape(8, 2, 8, 8, 128), axis=(0, 2))
    return total.reshape(2, 2, 2, 256).transpose(1, 2, 0, 3).reshape(2, 1024)


def solution(mesh):
    fine = Mesh(mesh.devices.reshape(2, 2, 8, 2, 8), ("xh", "core", "z", "xl", "y"))
    rows = P(("xh", "core", "z", "xl", "y"), None)
    in_specs = (rows, P(("z", "xl", "y"), ("xh", "core")))
    return jax.shard_map(shards, mesh=fine, in_specs=in_specs, out_specs=rows, check_vma=False)
```

```python
import jax
import jax.numpy as jnp
from jax import lax
from jax.experimental import pallas as pl
from jax.experimental.pallas import tpu as pltpu
from jax.sharding import Mesh, PartitionSpec as P

RING = ("xh", "xl")
RIGHT = [(i, (i + 1) % 4) for i in range(4)]
LEFT = [(i, (i + 3) % 4) for i in range(4)]
SWAP = [(0, 1), (1, 0)]
VMEM = pl.BlockSpec(memory_space=pltpu.VMEM)
LIMIT = 20 * 2**20
H_LIMIT = 8 * 2**20
SPLIT = 1920
G_FLOPS = 2 * 10**10
B_FLOPS = 10**9
FLOPS = 10**11
N_FLOPS = 4 * 10**9


def keep(*refs):
    for source, target in zip(refs[: len(refs) // 2], refs[len(refs) // 2 :]):
        target[...] = source[...]


def kept(flops, *pieces):
    return pl.pallas_call(
        keep,
        out_shape=[jax.ShapeDtypeStruct(piece.shape, piece.dtype) for piece in pieces],
        in_specs=[VMEM] * len(pieces),
        out_specs=[VMEM] * len(pieces),
        compiler_params=pltpu.CompilerParams(vmem_limit_bytes=H_LIMIT),
        cost_estimate=pl.CostEstimate(flops=flops, bytes_accessed=2**21, transcendentals=0),
    )(*pieces)


def halves(blocks, top_ref, low_ref):
    top_ref[...] = blocks[:SPLIT]
    low_ref[...] = blocks[SPLIT:]


def halved(blocks):
    return pl.pallas_call(
        halves,
        out_shape=[jax.ShapeDtypeStruct((rows, 256), jnp.bfloat16) for rows in (SPLIT, 2560 - SPLIT)],
        in_specs=[VMEM],
        out_specs=[VMEM, VMEM],
        compiler_params=pltpu.CompilerParams(vmem_limit_bytes=H_LIMIT),
    )(blocks)


def times(rows, halves):
    top = jnp.dot(rows[:, :SPLIT], halves[0][...], preferred_element_type=jnp.float32)
    return top + jnp.dot(rows[:, SPLIT:], halves[1][...], preferred_element_type=jnp.float32)


def place():
    xh, xl = lax.axis_index("xh"), lax.axis_index("xl")
    return xh, lax.rem(xh + xl, 2), lax.rem(xh + 1 - xl, 2)


def same():
    return lax.axis_index("xl") == lax.axis_index("core")


def own_near(pieces, *refs):
    here, left, right, rows, sum_ref = refs[:2], refs[2:4], refs[4:6], refs[6], refs[7]
    xh, right_xh, left_xh = place()
    rows[...] = pieces[...].reshape(256, 2560)

    @pl.when(same())
    def _():
        sum_ref[xh] = times(rows, here)
        sum_ref[1 - xh] = jnp.zeros((256, 256), jnp.float32)

    @pl.when(jnp.logical_not(same()))
    def _():
        sum_ref[right_xh] = times(rows, right)
        sum_ref[left_xh] = times(rows, left)


def other_near(first_ref, pieces, *refs):
    here, left, right, rows, sum_ref = refs[:2], refs[2:4], refs[4:6], refs[6], refs[7]
    xh, right_xh, left_xh = place()
    rows[...] = pieces[...].reshape(256, 2560)

    @pl.when(same())
    def _():
        sum_ref[right_xh] = first_ref[right_xh] + times(rows, right)
        sum_ref[left_xh] = first_ref[left_xh] + times(rows, left)

    @pl.when(jnp.logical_not(same()))
    def _():
        sum_ref[xh] = first_ref[xh] + times(rows, here)
        sum_ref[1 - xh] = first_ref[1 - xh]


def with_far(near_ref, own, other, far_top, far_low, out_ref, sum_ref):
    xh = lax.axis_index("xh")
    sum_ref[xh] = near_ref[xh]

    @pl.when(same())
    def _():
        sum_ref[1 - xh] = near_ref[1 - xh] + times(own, (far_top, far_low))

    @pl.when(jnp.logical_not(same()))
    def _():
        sum_ref[1 - xh] = near_ref[1 - xh] + times(other, (far_top, far_low))

    for block in range(2):
        for half in range(2):
            out_ref[pl.ds(2 * block + half, 256, stride=4), :] = sum_ref[block, :, 128 * half : 128 * half + 128]


SUMS = jax.ShapeDtypeStruct((2, 256, 256), jnp.float32)
ROWS = jax.ShapeDtypeStruct((256, 2560), jnp.bfloat16)


def run(kernel, flops, outs, scratch, *operands):
    return pl.pallas_call(
        kernel,
        out_shape=outs,
        in_specs=[VMEM] * len(operands),
        out_specs=[VMEM] * len(outs),
        scratch_shapes=scratch,
        compiler_params=pltpu.CompilerParams(vmem_limit_bytes=LIMIT),
        cost_estimate=pl.CostEstimate(flops=flops, bytes_accessed=2**22, transcendentals=0),
    )(*operands)


def shards(amplitudes, integrals):
    top, low = halved(integrals)
    left_top = lax.ppermute(top, RING, RIGHT)
    right_low = lax.ppermute(low, RING, LEFT)
    left_low = lax.ppermute(low, RING, RIGHT)
    right_top = lax.ppermute(top, RING, LEFT)
    (left_top,) = kept(G_FLOPS, left_top)
    (right_low,) = kept(B_FLOPS, right_low)
    far_top = lax.ppermute(left_top, RING, RIGHT)
    far_low = lax.ppermute(right_low, RING, LEFT)
    raw = lax.all_to_all(amplitudes.reshape(2, 128, 2560), ("z", "core", "y"), split_axis=1, concat_axis=1, tiled=True)
    raw, _, _ = lax.optimization_barrier((raw, left_top, right_low))
    raw_other = lax.ppermute(raw, "core", SWAP)
    near = (top, low, left_top, left_low, right_top, right_low)
    own, first = run(own_near, FLOPS, [ROWS, SUMS], [], raw.transpose(1, 0, 2), *near)
    other, second = run(other_near, N_FLOPS, [ROWS, SUMS], [], first, raw_other.transpose(1, 0, 2), *near)
    partial = jax.ShapeDtypeStruct((1024, 128), jnp.float32)
    scratch = [pltpu.VMEM((2, 256, 256), jnp.float32)]
    (partial,) = run(with_far, 10**9, [partial], scratch, second, own, other, far_top, far_low)
    partial = partial.reshape(128, 8, 128)
    parts = lax.all_to_all(partial, ("z", "core", "y"), split_axis=0, concat_axis=0, tiled=True)
    total = 0.5 * jnp.sum(parts.reshape(8, 2, 8, 8, 128), axis=(0, 2))
    return total.reshape(2, 2, 2, 256).transpose(1, 2, 0, 3).reshape(2, 1024)


def solution(mesh):
    fine = Mesh(mesh.devices.reshape(2, 2, 8, 2, 8), ("xh", "core", "z", "xl", "y"))
    rows = P(("xh", "core", "z", "xl", "y"), None)
    in_specs = (rows, P(("z", "xl", "y"), ("xh", "core")))
    return jax.shard_map(shards, mesh=fine, in_specs=in_specs, out_specs=rows, check_vma=False)
```

```python
import jax
import jax.numpy as jnp
from jax import lax
from jax.experimental import pallas as pl
from jax.experimental.pallas import tpu as pltpu
from jax.sharding import Mesh, PartitionSpec as P

RING = ("xh", "xl")
RIGHT = [(i, (i + 1) % 4) for i in range(4)]
LEFT = [(i, (i + 3) % 4) for i in range(4)]
SWAP = [(0, 1), (1, 0)]
VMEM = pl.BlockSpec(memory_space=pltpu.VMEM)
LIMIT = 20 * 2**20
H_LIMIT = 8 * 2**20
SPLIT = 1792
G_FLOPS = 18 * 10**9
B_FLOPS = 10**9
FLOPS = 10**11
N_FLOPS = 4 * 10**9


def keep(*refs):
    for source, target in zip(refs[: len(refs) // 2], refs[len(refs) // 2 :]):
        target[...] = source[: target.shape[0]]


def kept(flops, *pieces, rows=None):
    return pl.pallas_call(
        keep,
        out_shape=[jax.ShapeDtypeStruct((rows or piece.shape[0], 256), piece.dtype) for piece in pieces],
        in_specs=[VMEM] * len(pieces),
        out_specs=[VMEM] * len(pieces),
        compiler_params=pltpu.CompilerParams(vmem_limit_bytes=H_LIMIT),
        cost_estimate=pl.CostEstimate(flops=flops, bytes_accessed=2**21, transcendentals=0),
    )(*pieces)


def halves(blocks, top_ref, low_ref):
    top_ref[...] = blocks[:SPLIT]
    low_ref[...] = blocks[SPLIT:]


def halved(blocks):
    return pl.pallas_call(
        halves,
        out_shape=[jax.ShapeDtypeStruct((rows, 256), jnp.bfloat16) for rows in (SPLIT, 2560 - SPLIT)],
        in_specs=[VMEM],
        out_specs=[VMEM, VMEM],
        compiler_params=pltpu.CompilerParams(vmem_limit_bytes=H_LIMIT),
    )(blocks)


def times(rows, halves):
    if len(halves) == 1:
        return jnp.dot(rows[...], halves[0][...], preferred_element_type=jnp.float32)
    top = jnp.dot(rows[:, :SPLIT], halves[0][...], preferred_element_type=jnp.float32)
    return top + jnp.dot(rows[:, SPLIT:], halves[1][...], preferred_element_type=jnp.float32)


def place():
    xh, xl = lax.axis_index("xh"), lax.axis_index("xl")
    return xh, lax.rem(xh + xl, 2), lax.rem(xh + 1 - xl, 2)


def same():
    return lax.axis_index("xl") == lax.axis_index("core")


def own_near(pieces, *refs):
    here, left, right, rows, sum_ref = refs[:1], refs[1:2], refs[2:4], refs[4], refs[5]
    xh, right_xh, left_xh = place()
    rows[...] = pieces[...].reshape(256, 2560)

    @pl.when(same())
    def _():
        sum_ref[xh] = times(rows, here)
        sum_ref[1 - xh] = jnp.zeros((256, 256), jnp.float32)

    @pl.when(jnp.logical_not(same()))
    def _():
        sum_ref[right_xh] = times(rows, right)
        sum_ref[left_xh] = times(rows, left)


def other_near(first_ref, pieces, *refs):
    here, left, right, rows, sum_ref = refs[:1], refs[1:2], refs[2:4], refs[4], refs[5]
    xh, right_xh, left_xh = place()
    rows[...] = pieces[...].reshape(256, 2560)

    @pl.when(same())
    def _():
        sum_ref[right_xh] = first_ref[right_xh] + times(rows, right)
        sum_ref[left_xh] = first_ref[left_xh] + times(rows, left)

    @pl.when(jnp.logical_not(same()))
    def _():
        sum_ref[xh] = first_ref[xh] + times(rows, here)
        sum_ref[1 - xh] = first_ref[1 - xh]


def with_far(near_ref, own, other, far_top, far_low, out_ref, sum_ref):
    xh = lax.axis_index("xh")
    sum_ref[xh] = near_ref[xh]

    @pl.when(same())
    def _():
        sum_ref[1 - xh] = near_ref[1 - xh] + times(own, (far_top, far_low))

    @pl.when(jnp.logical_not(same()))
    def _():
        sum_ref[1 - xh] = near_ref[1 - xh] + times(other, (far_top, far_low))

    for block in range(2):
        for half in range(2):
            out_ref[pl.ds(2 * block + half, 256, stride=4), :] = sum_ref[block, :, 128 * half : 128 * half + 128]


SUMS = jax.ShapeDtypeStruct((2, 256, 256), jnp.float32)
ROWS = jax.ShapeDtypeStruct((256, 2560), jnp.bfloat16)


def run(kernel, flops, outs, scratch, *operands):
    return pl.pallas_call(
        kernel,
        out_shape=outs,
        in_specs=[VMEM] * len(operands),
        out_specs=[VMEM] * len(outs),
        scratch_shapes=scratch,
        compiler_params=pltpu.CompilerParams(vmem_limit_bytes=LIMIT),
        cost_estimate=pl.CostEstimate(flops=flops, bytes_accessed=2**22, transcendentals=0),
    )(*operands)


def shards(amplitudes, integrals):
    top, low = halved(integrals)
    left = lax.ppermute(integrals, RING, RIGHT)
    right_low = lax.ppermute(low, RING, LEFT)
    right_top = lax.ppermute(top, RING, LEFT)
    (left_top,) = kept(G_FLOPS, left, rows=SPLIT)
    (right_low,) = kept(B_FLOPS, right_low)
    far_top = lax.ppermute(left_top, RING, RIGHT)
    far_low = lax.ppermute(right_low, RING, LEFT)
    raw = lax.all_to_all(amplitudes.reshape(2, 128, 2560), ("z", "core", "y"), split_axis=1, concat_axis=1, tiled=True)
    raw, _, _ = lax.optimization_barrier((raw, left_top, right_low))
    raw_other = lax.ppermute(raw, "core", SWAP)
    near = (integrals, left, right_top, right_low)
    own, first = run(own_near, FLOPS, [ROWS, SUMS], [], raw.transpose(1, 0, 2), *near)
    other, second = run(other_near, N_FLOPS, [ROWS, SUMS], [], first, raw_other.transpose(1, 0, 2), *near)
    partial = jax.ShapeDtypeStruct((1024, 128), jnp.float32)
    scratch = [pltpu.VMEM((2, 256, 256), jnp.float32)]
    (partial,) = run(with_far, 10**9, [partial], scratch, second, own, other, far_top, far_low)
    partial = partial.reshape(128, 8, 128)
    parts = lax.all_to_all(partial, ("z", "core", "y"), split_axis=0, concat_axis=0, tiled=True)
    total = 0.5 * jnp.sum(parts.reshape(8, 2, 8, 8, 128), axis=(0, 2))
    return total.reshape(2, 2, 2, 256).transpose(1, 2, 0, 3).reshape(2, 1024)


def solution(mesh):
    fine = Mesh(mesh.devices.reshape(2, 2, 8, 2, 8), ("xh", "core", "z", "xl", "y"))
    rows = P(("xh", "core", "z", "xl", "y"), None)
    in_specs = (rows, P(("z", "xl", "y"), ("xh", "core")))
    return jax.shard_map(shards, mesh=fine, in_specs=in_specs, out_specs=rows, check_vma=False)
```

```python
import jax
import jax.numpy as jnp
from jax import lax
from jax.experimental import pallas as pl
from jax.experimental.pallas import tpu as pltpu
from jax.sharding import Mesh, PartitionSpec as P

RING = ("xh", "xl")
RIGHT = [(i, (i + 1) % 4) for i in range(4)]
LEFT = [(i, (i + 3) % 4) for i in range(4)]
SWAP = [(0, 1), (1, 0)]
VMEM = pl.BlockSpec(memory_space=pltpu.VMEM)
ANY = pl.BlockSpec(memory_space=pl.ANY)
LIMIT = 20 * 2**20
H_LIMIT = 8 * 2**20
SPLIT = 1920
G_FLOPS = 18 * 10**9
FLOPS = 10**11
N_FLOPS = 4 * 10**9


def keep(left, top_ref, sem):
    top = pltpu.make_async_copy(left.at[:SPLIT], top_ref, sem)
    top.start()
    top.wait()


def kept(left):
    return pl.pallas_call(
        keep,
        out_shape=jax.ShapeDtypeStruct((SPLIT, 256), jnp.bfloat16),
        in_specs=[ANY],
        out_specs=VMEM,
        scratch_shapes=[pltpu.SemaphoreType.DMA],
        compiler_params=pltpu.CompilerParams(vmem_limit_bytes=H_LIMIT),
        cost_estimate=pl.CostEstimate(flops=G_FLOPS, bytes_accessed=2**21, transcendentals=0),
    )(left)


def halves(blocks, top_ref, low_ref):
    top_ref[...] = blocks[:SPLIT]
    low_ref[...] = blocks[SPLIT:]


def halved(blocks):
    return pl.pallas_call(
        halves,
        out_shape=[jax.ShapeDtypeStruct((rows, 256), jnp.bfloat16) for rows in (SPLIT, 2560 - SPLIT)],
        in_specs=[VMEM],
        out_specs=[VMEM, VMEM],
        compiler_params=pltpu.CompilerParams(vmem_limit_bytes=H_LIMIT),
    )(blocks)


def times(rows, halves):
    if len(halves) == 1:
        return jnp.dot(rows[...], halves[0][...], preferred_element_type=jnp.float32)
    top = jnp.dot(rows[:, :SPLIT], halves[0][...], preferred_element_type=jnp.float32)
    return top + jnp.dot(rows[:, SPLIT:], halves[1][...], preferred_element_type=jnp.float32)


def place():
    xh, xl = lax.axis_index("xh"), lax.axis_index("xl")
    return xh, lax.rem(xh + xl, 2), lax.rem(xh + 1 - xl, 2)


def same():
    return lax.axis_index("xl") == lax.axis_index("core")


def own_near(pieces, *refs):
    here, left, right, rows, sum_ref = refs[:1], refs[1:2], refs[2:4], refs[4], refs[5]
    xh, right_xh, left_xh = place()
    rows[...] = pieces[...].reshape(256, 2560)

    @pl.when(same())
    def _():
        sum_ref[xh] = times(rows, here)
        sum_ref[1 - xh] = jnp.zeros((256, 256), jnp.float32)

    @pl.when(jnp.logical_not(same()))
    def _():
        sum_ref[right_xh] = times(rows, right)
        sum_ref[left_xh] = times(rows, left)


def other_near(first_ref, pieces, *refs):
    here, left, right, rows, sum_ref = refs[:1], refs[1:2], refs[2:4], refs[4], refs[5]
    xh, right_xh, left_xh = place()
    rows[...] = pieces[...].reshape(256, 2560)

    @pl.when(same())
    def _():
        sum_ref[right_xh] = first_ref[right_xh] + times(rows, right)
        sum_ref[left_xh] = first_ref[left_xh] + times(rows, left)

    @pl.when(jnp.logical_not(same()))
    def _():
        sum_ref[xh] = first_ref[xh] + times(rows, here)
        sum_ref[1 - xh] = first_ref[1 - xh]


def with_far(near_ref, own, other, far_top, far_low, out_ref, sum_ref):
    xh = lax.axis_index("xh")
    sum_ref[xh] = near_ref[xh]

    @pl.when(same())
    def _():
        sum_ref[1 - xh] = near_ref[1 - xh] + times(own, (far_top, far_low))

    @pl.when(jnp.logical_not(same()))
    def _():
        sum_ref[1 - xh] = near_ref[1 - xh] + times(other, (far_top, far_low))

    for block in range(2):
        for half in range(2):
            out_ref[pl.ds(2 * block + half, 256, stride=4), :] = sum_ref[block, :, 128 * half : 128 * half + 128]


SUMS = jax.ShapeDtypeStruct((2, 256, 256), jnp.float32)
ROWS = jax.ShapeDtypeStruct((256, 2560), jnp.bfloat16)


def run(kernel, flops, outs, scratch, *operands):
    return pl.pallas_call(
        kernel,
        out_shape=outs,
        in_specs=[VMEM] * len(operands),
        out_specs=[VMEM] * len(outs),
        scratch_shapes=scratch,
        compiler_params=pltpu.CompilerParams(vmem_limit_bytes=LIMIT),
        cost_estimate=pl.CostEstimate(flops=flops, bytes_accessed=2**22, transcendentals=0),
    )(*operands)


def shards(amplitudes, integrals):
    top, low = halved(integrals)
    left = lax.ppermute(integrals, RING, RIGHT)
    right_low = lax.ppermute(low, RING, LEFT)
    right_top = lax.ppermute(top, RING, LEFT)
    left_top = kept(left)
    far_top = lax.ppermute(left_top, RING, RIGHT)
    far_low = lax.ppermute(right_low, RING, LEFT)
    raw = lax.all_to_all(amplitudes.reshape(2, 128, 2560), ("z", "core", "y"), split_axis=1, concat_axis=1, tiled=True)
    raw, _ = lax.optimization_barrier((raw, left_top))
    raw_other = lax.ppermute(raw, "core", SWAP)
    near = (integrals, left, right_top, right_low)
    own, first = run(own_near, FLOPS, [ROWS, SUMS], [], raw.transpose(1, 0, 2), *near)
    other, second = run(other_near, N_FLOPS, [ROWS, SUMS], [], first, raw_other.transpose(1, 0, 2), *near)
    partial = jax.ShapeDtypeStruct((1024, 128), jnp.float32)
    scratch = [pltpu.VMEM((2, 256, 256), jnp.float32)]
    (partial,) = run(with_far, 10**9, [partial], scratch, second, own, other, far_top, far_low)
    partial = partial.reshape(128, 8, 128)
    parts = lax.all_to_all(partial, ("z", "core", "y"), split_axis=0, concat_axis=0, tiled=True)
    total = 0.5 * jnp.sum(parts.reshape(8, 2, 8, 8, 128), axis=(0, 2))
    return total.reshape(2, 2, 2, 256).transpose(1, 2, 0, 3).reshape(2, 1024)


def solution(mesh):
    fine = Mesh(mesh.devices.reshape(2, 2, 8, 2, 8), ("xh", "core", "z", "xl", "y"))
    rows = P(("xh", "core", "z", "xl", "y"), None)
    in_specs = (rows, P(("z", "xl", "y"), ("xh", "core")))
    return jax.shard_map(shards, mesh=fine, in_specs=in_specs, out_specs=rows, check_vma=False)
```

```python
import jax
import jax.numpy as jnp
from jax import lax
from jax.experimental import pallas as pl
from jax.experimental.pallas import tpu as pltpu
from jax.sharding import Mesh, PartitionSpec as P

RING = ("xh", "xl")
RIGHT = [(i, (i + 1) % 4) for i in range(4)]
LEFT = [(i, (i + 3) % 4) for i in range(4)]
SWAP = [(0, 1), (1, 0)]
VMEM = pl.BlockSpec(memory_space=pltpu.VMEM)
ANY = pl.BlockSpec(memory_space=pl.ANY)
LIMIT = 20 * 2**20
H_LIMIT = 8 * 2**20
SPLIT = 1792
G_FLOPS = 18 * 10**9
FLOPS = 10**11
N_FLOPS = 4 * 10**9


def keep(left, top_ref, sem):
    top = pltpu.make_async_copy(left.at[:SPLIT], top_ref, sem)
    top.start()
    top.wait()


def kept(left):
    return pl.pallas_call(
        keep,
        out_shape=jax.ShapeDtypeStruct((SPLIT, 256), jnp.bfloat16),
        in_specs=[ANY],
        out_specs=VMEM,
        scratch_shapes=[pltpu.SemaphoreType.DMA],
        compiler_params=pltpu.CompilerParams(vmem_limit_bytes=H_LIMIT),
        cost_estimate=pl.CostEstimate(flops=G_FLOPS, bytes_accessed=2**21, transcendentals=0),
    )(left)


def halves(blocks, top_ref, low_ref):
    top_ref[...] = blocks[:SPLIT]
    low_ref[...] = blocks[SPLIT:]


def halved(blocks):
    return pl.pallas_call(
        halves,
        out_shape=[jax.ShapeDtypeStruct((rows, 256), jnp.bfloat16) for rows in (SPLIT, 2560 - SPLIT)],
        in_specs=[VMEM],
        out_specs=[VMEM, VMEM],
        compiler_params=pltpu.CompilerParams(vmem_limit_bytes=H_LIMIT),
    )(blocks)


def times(rows, halves):
    if len(halves) == 1:
        return jnp.dot(rows[...], halves[0][...], preferred_element_type=jnp.float32)
    top = jnp.dot(rows[:, :SPLIT], halves[0][...], preferred_element_type=jnp.float32)
    return top + jnp.dot(rows[:, SPLIT:], halves[1][...], preferred_element_type=jnp.float32)


def place():
    xh, xl = lax.axis_index("xh"), lax.axis_index("xl")
    return xh, lax.rem(xh + xl, 2), lax.rem(xh + 1 - xl, 2)


def same():
    return lax.axis_index("xl") == lax.axis_index("core")


def own_near(pieces, *refs):
    here, left, right, rows, sum_ref = refs[:1], refs[1:2], refs[2:4], refs[4], refs[5]
    xh, right_xh, left_xh = place()
    rows[...] = pieces[...].reshape(256, 2560)

    @pl.when(same())
    def _():
        sum_ref[xh] = times(rows, here)
        sum_ref[1 - xh] = jnp.zeros((256, 256), jnp.float32)

    @pl.when(jnp.logical_not(same()))
    def _():
        sum_ref[right_xh] = times(rows, right)
        sum_ref[left_xh] = times(rows, left)


def other_near(first_ref, pieces, *refs):
    here, left, right, rows, sum_ref = refs[:1], refs[1:2], refs[2:4], refs[4], refs[5]
    xh, right_xh, left_xh = place()
    rows[...] = pieces[...].reshape(256, 2560)

    @pl.when(same())
    def _():
        sum_ref[right_xh] = first_ref[right_xh] + times(rows, right)
        sum_ref[left_xh] = first_ref[left_xh] + times(rows, left)

    @pl.when(jnp.logical_not(same()))
    def _():
        sum_ref[xh] = first_ref[xh] + times(rows, here)
        sum_ref[1 - xh] = first_ref[1 - xh]


def with_far(near_ref, own, other, far_top, far_low, out_ref, sum_ref):
    xh = lax.axis_index("xh")
    sum_ref[xh] = near_ref[xh]

    @pl.when(same())
    def _():
        sum_ref[1 - xh] = near_ref[1 - xh] + times(own, (far_top, far_low))

    @pl.when(jnp.logical_not(same()))
    def _():
        sum_ref[1 - xh] = near_ref[1 - xh] + times(other, (far_top, far_low))

    for block in range(2):
        total = sum_ref[block].reshape(8, 2, 16, 256)
        for core in range(2):
            for half in range(2):
                piece = total[:, core, :, 128 * half : 128 * half + 128].reshape(128, 128)
                out_ref[pl.ds(512 * core + 2 * block + half, 128, stride=4), :] = piece


SUMS = jax.ShapeDtypeStruct((2, 256, 256), jnp.float32)
ROWS = jax.ShapeDtypeStruct((256, 2560), jnp.bfloat16)


def run(kernel, flops, outs, scratch, *operands):
    return pl.pallas_call(
        kernel,
        out_shape=outs,
        in_specs=[VMEM] * len(operands),
        out_specs=[VMEM] * len(outs),
        scratch_shapes=scratch,
        compiler_params=pltpu.CompilerParams(vmem_limit_bytes=LIMIT),
        cost_estimate=pl.CostEstimate(flops=flops, bytes_accessed=2**22, transcendentals=0),
    )(*operands)


def shards(amplitudes, integrals):
    top, low = halved(integrals)
    left = lax.ppermute(integrals, RING, RIGHT)
    right_low = lax.ppermute(low, RING, LEFT)
    right_top = lax.ppermute(top, RING, LEFT)
    left_top = kept(left)
    far_top = lax.ppermute(left_top, RING, RIGHT)
    far_low = lax.ppermute(right_low, RING, LEFT)
    raw = lax.all_to_all(amplitudes.reshape(2, 128, 2560), ("z", "core", "y"), split_axis=1, concat_axis=1, tiled=True)
    raw, _ = lax.optimization_barrier((raw, left_top))
    raw_other = lax.ppermute(raw, "core", SWAP)
    near = (integrals, left, right_top, right_low)
    own, first = run(own_near, FLOPS, [ROWS, SUMS], [], raw.transpose(1, 0, 2), *near)
    other, second = run(other_near, N_FLOPS, [ROWS, SUMS], [], first, raw_other.transpose(1, 0, 2), *near)
    partial = jax.ShapeDtypeStruct((1024, 128), jnp.float32)
    scratch = [pltpu.VMEM((2, 256, 256), jnp.float32)]
    (partial,) = run(with_far, 10**9, [partial], scratch, second, own, other, far_top, far_low)
    partial = partial.reshape(128, 8, 128)
    parts = lax.all_to_all(partial, ("core", "z", "y"), split_axis=0, concat_axis=0, tiled=True)
    total = 0.5 * jnp.sum(parts.reshape(2, 64, 8, 128), axis=1)
    return total.reshape(2, 2, 2, 256).transpose(1, 2, 0, 3).reshape(2, 1024)


def solution(mesh):
    fine = Mesh(mesh.devices.reshape(2, 2, 8, 2, 8), ("xh", "core", "z", "xl", "y"))
    rows = P(("xh", "core", "z", "xl", "y"), None)
    in_specs = (rows, P(("z", "xl", "y"), ("xh", "core")))
    return jax.shard_map(shards, mesh=fine, in_specs=in_specs, out_specs=rows, check_vma=False)
```

```python
import jax
import jax.numpy as jnp
from jax import lax
from jax.experimental import pallas as pl
from jax.experimental.pallas import tpu as pltpu
from jax.sharding import Mesh, PartitionSpec as P

RING = ("xh", "xl")
RIGHT = [(i, (i + 1) % 4) for i in range(4)]
LEFT = [(i, (i + 3) % 4) for i in range(4)]
SWAP = [(0, 1), (1, 0)]
VMEM = pl.BlockSpec(memory_space=pltpu.VMEM)
ANY = pl.BlockSpec(memory_space=pl.ANY)
LIMIT = 20 * 2**20
H_LIMIT = 8 * 2**20
SPLIT = 1792
G_FLOPS = 18 * 10**9
FLOPS = 10**11
L_FLOPS = 10**9
B_FLOPS = 10**9
N_FLOPS = 4 * 10**9


def keep(left, top_ref, sem):
    top = pltpu.make_async_copy(left.at[:SPLIT], top_ref, sem)
    top.start()
    top.wait()


def kept(left):
    return pl.pallas_call(
        keep,
        out_shape=jax.ShapeDtypeStruct((SPLIT, 256), jnp.bfloat16),
        in_specs=[ANY],
        out_specs=VMEM,
        scratch_shapes=[pltpu.SemaphoreType.DMA],
        compiler_params=pltpu.CompilerParams(vmem_limit_bytes=H_LIMIT),
        cost_estimate=pl.CostEstimate(flops=G_FLOPS, bytes_accessed=2**21, transcendentals=0),
    )(left)


def follow(right_low, left_top, low_ref):
    low_ref[...] = right_low[...]


def followed(right_low, left_top):
    return pl.pallas_call(
        follow,
        out_shape=jax.ShapeDtypeStruct(right_low.shape, right_low.dtype),
        in_specs=[VMEM, ANY],
        out_specs=VMEM,
        compiler_params=pltpu.CompilerParams(vmem_limit_bytes=H_LIMIT),
        cost_estimate=pl.CostEstimate(flops=B_FLOPS, bytes_accessed=2**20, transcendentals=0),
    )(right_low, left_top)


def halves(blocks, top_ref, low_ref):
    top_ref[...] = blocks[:SPLIT]
    low_ref[...] = blocks[SPLIT:]


def halved(blocks):
    return pl.pallas_call(
        halves,
        out_shape=[jax.ShapeDtypeStruct((rows, 256), jnp.bfloat16) for rows in (SPLIT, 2560 - SPLIT)],
        in_specs=[VMEM],
        out_specs=[VMEM, VMEM],
        compiler_params=pltpu.CompilerParams(vmem_limit_bytes=H_LIMIT),
    )(blocks)


def times(rows, halves):
    if len(halves) == 1:
        return jnp.dot(rows[...], halves[0][...], preferred_element_type=jnp.float32)
    top = jnp.dot(rows[:, :SPLIT], halves[0][...], preferred_element_type=jnp.float32)
    return top + jnp.dot(rows[:, SPLIT:], halves[1][...], preferred_element_type=jnp.float32)


def place():
    xh, xl = lax.axis_index("xh"), lax.axis_index("xl")
    return xh, lax.rem(xh + xl, 2), lax.rem(xh + 1 - xl, 2)


def same():
    return lax.axis_index("xl") == lax.axis_index("core")


def own_near(pieces, *refs):
    here, left, right, rows, sum_ref = refs[:1], refs[1:2], refs[2:4], refs[4], refs[5]
    xh, right_xh, left_xh = place()
    rows[...] = pieces[...].reshape(256, 2560)

    @pl.when(same())
    def _():
        sum_ref[xh] = times(rows, here)
        sum_ref[1 - xh] = jnp.zeros((256, 256), jnp.float32)

    @pl.when(jnp.logical_not(same()))
    def _():
        sum_ref[right_xh] = times(rows, right)
        sum_ref[left_xh] = times(rows, left)


def other_near(first_ref, pieces, *refs):
    here, left, right, rows, sum_ref = refs[:1], refs[1:2], refs[2:4], refs[4], refs[5]
    xh, right_xh, left_xh = place()
    rows[...] = pieces[...].reshape(256, 2560)

    @pl.when(same())
    def _():
        sum_ref[right_xh] = first_ref[right_xh] + times(rows, right)
        sum_ref[left_xh] = first_ref[left_xh] + times(rows, left)

    @pl.when(jnp.logical_not(same()))
    def _():
        sum_ref[xh] = first_ref[xh] + times(rows, here)
        sum_ref[1 - xh] = first_ref[1 - xh]


def with_far_top(near_ref, own, other, far_top, sum_ref):
    xh = lax.axis_index("xh")
    sum_ref[xh] = near_ref[xh]

    @pl.when(same())
    def _():
        sum_ref[1 - xh] = near_ref[1 - xh] + jnp.dot(own[:, :SPLIT], far_top[...], preferred_element_type=jnp.float32)

    @pl.when(jnp.logical_not(same()))
    def _():
        sum_ref[1 - xh] = near_ref[1 - xh] + jnp.dot(other[:, :SPLIT], far_top[...], preferred_element_type=jnp.float32)


def with_far_low(most_ref, own, other, far_low, out_ref, sum_ref):
    xh = lax.axis_index("xh")
    sum_ref[xh] = most_ref[xh]

    @pl.when(same())
    def _():
        sum_ref[1 - xh] = most_ref[1 - xh] + jnp.dot(own[:, SPLIT:], far_low[...], preferred_element_type=jnp.float32)

    @pl.when(jnp.logical_not(same()))
    def _():
        sum_ref[1 - xh] = most_ref[1 - xh] + jnp.dot(other[:, SPLIT:], far_low[...], preferred_element_type=jnp.float32)

    for block in range(2):
        total = sum_ref[block].reshape(8, 2, 16, 256)
        for core in range(2):
            for half in range(2):
                piece = total[:, core, :, 128 * half : 128 * half + 128].reshape(128, 128)
                out_ref[pl.ds(512 * core + 2 * block + half, 128, stride=4), :] = piece


SUMS = jax.ShapeDtypeStruct((2, 256, 256), jnp.float32)
ROWS = jax.ShapeDtypeStruct((256, 2560), jnp.bfloat16)


def run(kernel, flops, outs, scratch, *operands):
    return pl.pallas_call(
        kernel,
        out_shape=outs,
        in_specs=[VMEM] * len(operands),
        out_specs=[VMEM] * len(outs),
        scratch_shapes=scratch,
        compiler_params=pltpu.CompilerParams(vmem_limit_bytes=LIMIT),
        cost_estimate=pl.CostEstimate(flops=flops, bytes_accessed=2**22, transcendentals=0),
    )(*operands)


def shards(amplitudes, integrals):
    top, low = halved(integrals)
    left = lax.ppermute(integrals, RING, RIGHT)
    right_low = lax.ppermute(low, RING, LEFT)
    right_top = lax.ppermute(top, RING, LEFT)
    left_top = kept(left)
    right_low = followed(right_low, left_top)
    far_top = lax.ppermute(left_top, RING, RIGHT)
    far_low = lax.ppermute(right_low, RING, LEFT)
    raw = lax.all_to_all(amplitudes.reshape(2, 128, 2560), ("z", "core", "y"), split_axis=1, concat_axis=1, tiled=True)
    raw, _ = lax.optimization_barrier((raw, left_top))
    raw_other = lax.ppermute(raw, "core", SWAP)
    near = (integrals, left, right_top, right_low)
    own, first = run(own_near, FLOPS, [ROWS, SUMS], [], raw.transpose(1, 0, 2), *near)
    other, second = run(other_near, N_FLOPS, [ROWS, SUMS], [], first, raw_other.transpose(1, 0, 2), *near)
    partial = jax.ShapeDtypeStruct((1024, 128), jnp.float32)
    scratch = [pltpu.VMEM((2, 256, 256), jnp.float32)]
    (third,) = run(with_far_top, 10**9, [SUMS], [], second, own, other, far_top)
    (partial,) = run(with_far_low, L_FLOPS, [partial], scratch, third, own, other, far_low)
    partial = partial.reshape(128, 8, 128)
    parts = lax.all_to_all(partial, ("core", "z", "y"), split_axis=0, concat_axis=0, tiled=True)
    total = 0.5 * jnp.sum(parts.reshape(2, 64, 8, 128), axis=1)
    return total.reshape(2, 2, 2, 256).transpose(1, 2, 0, 3).reshape(2, 1024)


def solution(mesh):
    fine = Mesh(mesh.devices.reshape(2, 2, 8, 2, 8), ("xh", "core", "z", "xl", "y"))
    rows = P(("xh", "core", "z", "xl", "y"), None)
    in_specs = (rows, P(("z", "xl", "y"), ("xh", "core")))
    return jax.shard_map(shards, mesh=fine, in_specs=in_specs, out_specs=rows, check_vma=False)
```

```python
import jax
import jax.numpy as jnp
from jax import lax
from jax.experimental import pallas as pl
from jax.experimental.pallas import tpu as pltpu
from jax.sharding import Mesh, PartitionSpec as P

RING = ("xh", "xl")
RIGHT = [(i, (i + 1) % 4) for i in range(4)]
LEFT = [(i, (i + 3) % 4) for i in range(4)]
SWAP = [(0, 1), (1, 0)]
VMEM = pl.BlockSpec(memory_space=pltpu.VMEM)
ANY = pl.BlockSpec(memory_space=pl.ANY)
LIMIT = 20 * 2**20
H_LIMIT = 8 * 2**20
SPLIT = 1664
G_FLOPS = 18 * 10**9
FLOPS = 10**11
L_FLOPS = 10**9
B_FLOPS = 10**9
N_FLOPS = 4 * 10**9


def keep(left, top_ref, sem):
    top = pltpu.make_async_copy(left.at[:SPLIT], top_ref, sem)
    top.start()
    top.wait()


def kept(left):
    return pl.pallas_call(
        keep,
        out_shape=jax.ShapeDtypeStruct((SPLIT, 256), jnp.bfloat16),
        in_specs=[ANY],
        out_specs=VMEM,
        scratch_shapes=[pltpu.SemaphoreType.DMA],
        compiler_params=pltpu.CompilerParams(vmem_limit_bytes=H_LIMIT),
        cost_estimate=pl.CostEstimate(flops=G_FLOPS, bytes_accessed=2**21, transcendentals=0),
    )(left)


def follow(right_low, left_top, low_ref):
    low_ref[...] = right_low[...]


def followed(right_low, left_top):
    return pl.pallas_call(
        follow,
        out_shape=jax.ShapeDtypeStruct(right_low.shape, right_low.dtype),
        in_specs=[VMEM, ANY],
        out_specs=VMEM,
        compiler_params=pltpu.CompilerParams(vmem_limit_bytes=H_LIMIT),
        cost_estimate=pl.CostEstimate(flops=B_FLOPS, bytes_accessed=2**20, transcendentals=0),
    )(right_low, left_top)


def halves(blocks, top_ref, low_ref):
    top_ref[...] = blocks[:SPLIT]
    low_ref[...] = blocks[SPLIT:]


def halved(blocks):
    return pl.pallas_call(
        halves,
        out_shape=[jax.ShapeDtypeStruct((rows, 256), jnp.bfloat16) for rows in (SPLIT, 2560 - SPLIT)],
        in_specs=[VMEM],
        out_specs=[VMEM, VMEM],
        compiler_params=pltpu.CompilerParams(vmem_limit_bytes=H_LIMIT),
    )(blocks)


def times(rows, halves):
    if len(halves) == 1:
        return jnp.dot(rows[...], halves[0][...], preferred_element_type=jnp.float32)
    top = jnp.dot(rows[:, :SPLIT], halves[0][...], preferred_element_type=jnp.float32)
    return top + jnp.dot(rows[:, SPLIT:], halves[1][...], preferred_element_type=jnp.float32)


def place():
    xh, xl = lax.axis_index("xh"), lax.axis_index("xl")
    return xh, lax.rem(xh + xl, 2), lax.rem(xh + 1 - xl, 2)


def same():
    return lax.axis_index("xl") == lax.axis_index("core")


def own_near(pieces, *refs):
    here, left, right, rows, sum_ref = refs[:1], refs[1:2], refs[2:4], refs[4], refs[5]
    xh, right_xh, left_xh = place()
    rows[...] = pieces[...].reshape(256, 2560)

    @pl.when(same())
    def _():
        sum_ref[xh] = times(rows, here)
        sum_ref[1 - xh] = jnp.zeros((256, 256), jnp.float32)

    @pl.when(jnp.logical_not(same()))
    def _():
        sum_ref[right_xh] = times(rows, right)
        sum_ref[left_xh] = times(rows, left)


def other_near(first_ref, pieces, *refs):
    here, left, right, rows, sum_ref = refs[:1], refs[1:2], refs[2:4], refs[4], refs[5]
    xh, right_xh, left_xh = place()
    rows[...] = pieces[...].reshape(256, 2560)

    @pl.when(same())
    def _():
        sum_ref[right_xh] = first_ref[right_xh] + times(rows, right)
        sum_ref[left_xh] = first_ref[left_xh] + times(rows, left)

    @pl.when(jnp.logical_not(same()))
    def _():
        sum_ref[xh] = first_ref[xh] + times(rows, here)
        sum_ref[1 - xh] = first_ref[1 - xh]


def with_far_top(near_ref, own, other, far_top, sum_ref):
    xh = lax.axis_index("xh")
    sum_ref[xh] = near_ref[xh]

    @pl.when(same())
    def _():
        sum_ref[1 - xh] = near_ref[1 - xh] + jnp.dot(own[:, :SPLIT], far_top[...], preferred_element_type=jnp.float32)

    @pl.when(jnp.logical_not(same()))
    def _():
        sum_ref[1 - xh] = near_ref[1 - xh] + jnp.dot(other[:, :SPLIT], far_top[...], preferred_element_type=jnp.float32)


def with_far_low(most_ref, own, other, far_low, out_ref, sum_ref):
    xh = lax.axis_index("xh")
    sum_ref[xh] = most_ref[xh]

    @pl.when(same())
    def _():
        sum_ref[1 - xh] = most_ref[1 - xh] + jnp.dot(own[:, SPLIT:], far_low[...], preferred_element_type=jnp.float32)

    @pl.when(jnp.logical_not(same()))
    def _():
        sum_ref[1 - xh] = most_ref[1 - xh] + jnp.dot(other[:, SPLIT:], far_low[...], preferred_element_type=jnp.float32)

    for block in range(2):
        total = sum_ref[block].reshape(8, 2, 16, 256)
        for core in range(2):
            for half in range(2):
                piece = total[:, core, :, 128 * half : 128 * half + 128].reshape(128, 128)
                out_ref[pl.ds(512 * core + 2 * block + half, 128, stride=4), :] = piece


SUMS = jax.ShapeDtypeStruct((2, 256, 256), jnp.float32)
ROWS = jax.ShapeDtypeStruct((256, 2560), jnp.bfloat16)


def run(kernel, flops, outs, scratch, *operands):
    return pl.pallas_call(
        kernel,
        out_shape=outs,
        in_specs=[VMEM] * len(operands),
        out_specs=[VMEM] * len(outs),
        scratch_shapes=scratch,
        compiler_params=pltpu.CompilerParams(vmem_limit_bytes=LIMIT),
        cost_estimate=pl.CostEstimate(flops=flops, bytes_accessed=2**22, transcendentals=0),
    )(*operands)


def shards(amplitudes, integrals):
    top, low = halved(integrals)
    left = lax.ppermute(integrals, RING, RIGHT)
    right_low = lax.ppermute(low, RING, LEFT)
    right_top = lax.ppermute(top, RING, LEFT)
    left_top = kept(left)
    right_low = followed(right_low, left_top)
    far_top = lax.ppermute(left_top, RING, RIGHT)
    far_low = lax.ppermute(right_low, RING, LEFT)
    raw = lax.all_to_all(amplitudes.reshape(2, 128, 2560), ("z", "core", "y"), split_axis=1, concat_axis=1, tiled=True)
    raw, _ = lax.optimization_barrier((raw, left_top))
    raw_other = lax.ppermute(raw, "core", SWAP)
    near = (integrals, left, right_top, right_low)
    own, first = run(own_near, FLOPS, [ROWS, SUMS], [], raw.transpose(1, 0, 2), *near)
    other, second = run(other_near, N_FLOPS, [ROWS, SUMS], [], first, raw_other.transpose(1, 0, 2), *near)
    partial = jax.ShapeDtypeStruct((1024, 128), jnp.float32)
    scratch = [pltpu.VMEM((2, 256, 256), jnp.float32)]
    (third,) = run(with_far_top, 10**9, [SUMS], [], second, own, other, far_top)
    (partial,) = run(with_far_low, L_FLOPS, [partial], scratch, third, own, other, far_low)
    partial = partial.reshape(128, 8, 128)
    parts = lax.all_to_all(partial, ("core", "z", "y"), split_axis=0, concat_axis=0, tiled=True)
    total = 0.5 * jnp.sum(parts.reshape(2, 64, 8, 128), axis=1)
    return total.reshape(2, 2, 2, 256).transpose(1, 2, 0, 3).reshape(2, 1024)


def solution(mesh):
    fine = Mesh(mesh.devices.reshape(2, 2, 8, 2, 8), ("xh", "core", "z", "xl", "y"))
    rows = P(("xh", "core", "z", "xl", "y"), None)
    in_specs = (rows, P(("z", "xl", "y"), ("xh", "core")))
    return jax.shard_map(shards, mesh=fine, in_specs=in_specs, out_specs=rows, check_vma=False)
```

```python
import jax
import jax.numpy as jnp
from jax import lax
from jax.experimental import pallas as pl
from jax.experimental.pallas import tpu as pltpu
from jax.sharding import Mesh, PartitionSpec as P

RING = ("xh", "xl")
RIGHT = [(i, (i + 1) % 4) for i in range(4)]
LEFT = [(i, (i + 3) % 4) for i in range(4)]
SWAP = [(0, 1), (1, 0)]
VMEM = pl.BlockSpec(memory_space=pltpu.VMEM)
ANY = pl.BlockSpec(memory_space=pl.ANY)
LIMIT = 20 * 2**20
H_LIMIT = 8 * 2**20
SPLIT = 1792
G_FLOPS = 18 * 10**9
FLOPS = 10**11
L_FLOPS = 10**9
B_FLOPS = 10**9
N_FLOPS = 4 * 10**9


def keep(left, top_ref, passing, sems):
    rows = SPLIT // 4
    spans = [pl.ds(rows * n, rows) for n in range(4)]
    reads = [pltpu.make_async_copy(left.at[span], passing.at[n], sems.at[n]) for n, span in enumerate(spans)]
    writes = [pltpu.make_async_copy(passing.at[n], top_ref.at[span], sems.at[4 + n]) for n, span in enumerate(spans)]
    for read in reads:
        read.start()
    for read, write in zip(reads, writes):
        read.wait()
        write.start()
    for write in writes:
        write.wait()


def kept(left):
    return pl.pallas_call(
        keep,
        out_shape=jax.ShapeDtypeStruct((SPLIT, 256), jnp.bfloat16),
        in_specs=[ANY],
        out_specs=ANY,
        scratch_shapes=[pltpu.VMEM((4, SPLIT // 4, 256), jnp.bfloat16), pltpu.SemaphoreType.DMA((8,))],
        compiler_params=pltpu.CompilerParams(vmem_limit_bytes=H_LIMIT),
        cost_estimate=pl.CostEstimate(flops=G_FLOPS, bytes_accessed=2**21, transcendentals=0),
    )(left)


def follow(right_low, left_top, low_ref):
    low_ref[...] = right_low[...]


def followed(right_low, left_top):
    return pl.pallas_call(
        follow,
        out_shape=jax.ShapeDtypeStruct(right_low.shape, right_low.dtype),
        in_specs=[VMEM, ANY],
        out_specs=VMEM,
        compiler_params=pltpu.CompilerParams(vmem_limit_bytes=H_LIMIT),
        cost_estimate=pl.CostEstimate(flops=B_FLOPS, bytes_accessed=2**20, transcendentals=0),
    )(right_low, left_top)


def halves(blocks, top_ref, low_ref):
    top_ref[...] = blocks[:SPLIT]
    low_ref[...] = blocks[SPLIT:]


def halved(blocks):
    return pl.pallas_call(
        halves,
        out_shape=[jax.ShapeDtypeStruct((rows, 256), jnp.bfloat16) for rows in (SPLIT, 2560 - SPLIT)],
        in_specs=[VMEM],
        out_specs=[VMEM, VMEM],
        compiler_params=pltpu.CompilerParams(vmem_limit_bytes=H_LIMIT),
    )(blocks)


def times(rows, halves):
    if len(halves) == 1:
        return jnp.dot(rows[...], halves[0][...], preferred_element_type=jnp.float32)
    top = jnp.dot(rows[:, :SPLIT], halves[0][...], preferred_element_type=jnp.float32)
    return top + jnp.dot(rows[:, SPLIT:], halves[1][...], preferred_element_type=jnp.float32)


def place():
    xh, xl = lax.axis_index("xh"), lax.axis_index("xl")
    return xh, lax.rem(xh + xl, 2), lax.rem(xh + 1 - xl, 2)


def same():
    return lax.axis_index("xl") == lax.axis_index("core")


def own_near(pieces, *refs):
    here, left, right, rows, sum_ref = refs[:1], refs[1:2], refs[2:4], refs[4], refs[5]
    xh, right_xh, left_xh = place()
    rows[...] = pieces[...].reshape(256, 2560)

    @pl.when(same())
    def _():
        sum_ref[xh] = times(rows, here)
        sum_ref[1 - xh] = jnp.zeros((256, 256), jnp.float32)

    @pl.when(jnp.logical_not(same()))
    def _():
        sum_ref[right_xh] = times(rows, right)
        sum_ref[left_xh] = times(rows, left)


def other_near(first_ref, pieces, *refs):
    here, left, right, rows, sum_ref = refs[:1], refs[1:2], refs[2:4], refs[4], refs[5]
    xh, right_xh, left_xh = place()
    rows[...] = pieces[...].reshape(256, 2560)

    @pl.when(same())
    def _():
        sum_ref[right_xh] = first_ref[right_xh] + times(rows, right)
        sum_ref[left_xh] = first_ref[left_xh] + times(rows, left)

    @pl.when(jnp.logical_not(same()))
    def _():
        sum_ref[xh] = first_ref[xh] + times(rows, here)
        sum_ref[1 - xh] = first_ref[1 - xh]


def with_far_top(near_ref, own, other, far_top, sum_ref):
    xh = lax.axis_index("xh")
    sum_ref[xh] = near_ref[xh]

    @pl.when(same())
    def _():
        sum_ref[1 - xh] = near_ref[1 - xh] + jnp.dot(own[:, :SPLIT], far_top[...], preferred_element_type=jnp.float32)

    @pl.when(jnp.logical_not(same()))
    def _():
        sum_ref[1 - xh] = near_ref[1 - xh] + jnp.dot(other[:, :SPLIT], far_top[...], preferred_element_type=jnp.float32)


def with_far_low(most_ref, own, other, far_low, out_ref, sum_ref):
    xh = lax.axis_index("xh")
    sum_ref[xh] = most_ref[xh]

    @pl.when(same())
    def _():
        sum_ref[1 - xh] = most_ref[1 - xh] + jnp.dot(own[:, SPLIT:], far_low[...], preferred_element_type=jnp.float32)

    @pl.when(jnp.logical_not(same()))
    def _():
        sum_ref[1 - xh] = most_ref[1 - xh] + jnp.dot(other[:, SPLIT:], far_low[...], preferred_element_type=jnp.float32)

    for block in range(2):
        total = sum_ref[block].reshape(8, 2, 16, 256)
        for core in range(2):
            for half in range(2):
                piece = total[:, core, :, 128 * half : 128 * half + 128].reshape(128, 128)
                out_ref[pl.ds(512 * core + 2 * block + half, 128, stride=4), :] = piece


SUMS = jax.ShapeDtypeStruct((2, 256, 256), jnp.float32)
ROWS = jax.ShapeDtypeStruct((256, 2560), jnp.bfloat16)


def run(kernel, flops, outs, scratch, *operands):
    return pl.pallas_call(
        kernel,
        out_shape=outs,
        in_specs=[VMEM] * len(operands),
        out_specs=[VMEM] * len(outs),
        scratch_shapes=scratch,
        compiler_params=pltpu.CompilerParams(vmem_limit_bytes=LIMIT),
        cost_estimate=pl.CostEstimate(flops=flops, bytes_accessed=2**22, transcendentals=0),
    )(*operands)


def shards(amplitudes, integrals):
    top, low = halved(integrals)
    left = lax.ppermute(integrals, RING, RIGHT)
    right_low = lax.ppermute(low, RING, LEFT)
    right_top = lax.ppermute(top, RING, LEFT)
    left_top = kept(left)
    right_low = followed(right_low, left_top)
    far_top = lax.ppermute(left_top, RING, RIGHT)
    far_low = lax.ppermute(right_low, RING, LEFT)
    raw = lax.all_to_all(amplitudes.reshape(2, 128, 2560), ("z", "core", "y"), split_axis=1, concat_axis=1, tiled=True)
    raw, _ = lax.optimization_barrier((raw, left_top))
    raw_other = lax.ppermute(raw, "core", SWAP)
    near = (integrals, left, right_top, right_low)
    own, first = run(own_near, FLOPS, [ROWS, SUMS], [], raw.transpose(1, 0, 2), *near)
    other, second = run(other_near, N_FLOPS, [ROWS, SUMS], [], first, raw_other.transpose(1, 0, 2), *near)
    partial = jax.ShapeDtypeStruct((1024, 128), jnp.float32)
    scratch = [pltpu.VMEM((2, 256, 256), jnp.float32)]
    (third,) = run(with_far_top, 10**9, [SUMS], [], second, own, other, far_top)
    (partial,) = run(with_far_low, L_FLOPS, [partial], scratch, third, own, other, far_low)
    partial = partial.reshape(128, 8, 128)
    parts = lax.all_to_all(partial, ("core", "z", "y"), split_axis=0, concat_axis=0, tiled=True)
    total = 0.5 * jnp.sum(parts.reshape(2, 64, 8, 128), axis=1)
    return total.reshape(2, 2, 2, 256).transpose(1, 2, 0, 3).reshape(2, 1024)


def solution(mesh):
    fine = Mesh(mesh.devices.reshape(2, 2, 8, 2, 8), ("xh", "core", "z", "xl", "y"))
    rows = P(("xh", "core", "z", "xl", "y"), None)
    in_specs = (rows, P(("z", "xl", "y"), ("xh", "core")))
    return jax.shard_map(shards, mesh=fine, in_specs=in_specs, out_specs=rows, check_vma=False)
```
